32 devices in a mesh: ctx: 8 (over z, x), head: 4 (over y, core).
Axes of the slice: x: 2, y: 2, z: 4, core: 2. Of those that a mesh axis runs over, the one named last changes fastest.
Arguments:
- queries: bfloat16 [1024, 32, 128], P('ctx', 'head'), may hold values from -14 to 14
- keys: bfloat16 [1024, 32, 128], P('ctx', 'head'), may hold values from -14 to 14
- values: bfloat16 [1024, 32, 128], P('ctx', 'head'), may hold values from -6 to 6
- gain: float32 [32, 128], P('head'), may hold values from 0.1 to 1.9
- doc_lengths: int32 [8], replicated, may hold values from 1 to 256, 1024 in all
- cotangent: bfloat16 [1024, 32, 128], P('ctx', 'head'), may hold values from -6 to 6
Outputs:
- mixed: bfloat16 [1024, 32, 128], P('ctx', 'head')
- query_grad: bfloat16 [1024, 32, 128], P('ctx', 'head')
- key_grad: bfloat16 [1024, 32, 128], P('ctx', 'head')
- value_grad: bfloat16 [1024, 32, 128], P('ctx', 'head')
The draws below stay inside these ranges and needn't reach their ends.
All inputs are finite; a program needn't handle non-finite values.
Results may differ from the reference program's by a relative error of at most 0.0054.
Values may be sent and summed in bfloat16 or wider, within the bound.
A program may use at most 128 MiB of HBM per device.

```python
import math
import jax
import jax.numpy as jnp
import numpy as np
from jax import lax

HEADS = 32
DH = 128
TOK_DEV = 128
SPAN = 2
SEQ = 1024
MAXDOC = 256
NDOCS = 8


def draw_pair(key):
    shape = (SEQ, HEADS, DH)
    first, second = jax.random.split(jax.random.fold_in(key, 31), 2)
    query_drawn = jnp.clip(jax.random.normal(first, shape, jnp.float32), -6.0, 6.0)
    key_drawn = jnp.clip(jax.random.normal(second, shape, jnp.float32), -6.0, 6.0)
    return (query_drawn, key_drawn)


def draw_queries(key, part):
    return draw_pair(key)[0].astype(jnp.bfloat16)


def draw_keys(key, part):
    return draw_pair(key)[1].astype(jnp.bfloat16)


def block_scale(key, shape, cuts, smallest, top_value):
    def one(dim, blocks):
        draws = jax.random.uniform(jax.random.fold_in(jax.random.fold_in(key, 6), dim), (blocks,), jnp.float32, smallest / len(cuts), top_value / len(cuts))
        return jnp.repeat(jnp.exp(draws), shape[dim] // blocks).reshape((-1,) + (1,) * (len(shape) - dim - 1))

    level = one(*cuts[0])
    for cut in cuts[1:]:
        level = level * one(*cut)
    return level


def length_profile(amount, total, bound, slope):
    portions = [(1 << 20) // math.isqrt(rank ** slope) + 1 for rank in range(2, amount + 1)]
    spare, counts = total - bound - (amount - 1), [1] * (amount - 1)
    while spare > 0:
        candidates = [i for i in range(amount - 1) if counts[i] < bound]
        mass, left = sum([portions[i] for i in candidates]), spare
        for i in candidates:
            addition = min(bound - counts[i], max(1, left * portions[i] // mass), spare)
            counts[i] = counts[i] + addition
            spare = spare - addition
    return np.array([bound] + counts)


def uneven_parts(own_key, count, total, limit, skew):
    if count == 2:
        one = jax.random.randint(own_key, (), max(1, total - limit), min(limit, total - 1) + 1)
        return jnp.stack([one, total - one])
    lengths = jnp.asarray(length_profile(count, total, limit, skew), jnp.int32)
    pairs = (count - 1) // 2
    source_of, taker = lengths[1:1 + 2 * pairs:2], lengths[2:2 + 2 * pairs:2]
    margin = jnp.minimum(source_of - 1, limit - taker)
    moved = jax.random.randint(jax.random.fold_in(own_key, 1), (pairs,), 0, 1 << 20) % (margin + 1)
    lengths = lengths.at[1:1 + 2 * pairs:2].set(source_of - moved).at[2:2 + 2 * pairs:2].set(taker + moved)
    return lengths[jax.random.permutation(jax.random.fold_in(own_key, 2), count)]


def bell_draw(own_key, extent, deviation, limit, cuts=(), kind=jnp.bfloat16):
    result = deviation * jax.random.normal(own_key, extent, jnp.float32)
    if cuts:
        result = result * block_scale(own_key, extent, cuts, -0.22, 0.18)
    return jnp.clip(result, -limit, limit).astype(kind)


def setup_inputs(seed: int = 0) -> dict:
    key_of = jax.random.split(jax.random.key(seed), 7)
    queries = draw_queries(jax.random.fold_in(key_of[6], 71), 0)
    keys = draw_keys(jax.random.fold_in(key_of[6], 71), 0)
    values = bell_draw(key_of[2], (SEQ, HEADS, DH), 1.0, 6.0, ((0, 8), (1, 4)))
    gain = jnp.clip(1.0 + 0.18 * jax.random.normal(key_of[3], (HEADS, DH), jnp.float32), 0.1, 1.9)
    doc_lengths = uneven_parts(key_of[4], NDOCS, SEQ, MAXDOC, 2).astype(jnp.int32)
    cotangent = bell_draw(key_of[5], (SEQ, HEADS, DH), 1.0, 6.0, ((0, 8), (1, 4)))
    return dict(queries=queries, keys=keys, values=values, gain=gain, doc_lengths=doc_lengths, cotangent=cotangent)


neg_large = -1e+30
norm_eps = 1e-06

def wide(form, left, right):
    return jnp.einsum(form, left, right, precision=lax.Precision.HIGHEST)

def doc_index(doc_lengths, positions):
    starts = jnp.cumsum(doc_lengths) - doc_lengths
    return lax.optimization_barrier(jnp.sum((starts[None, :] <= positions[:, None]).astype(jnp.int32), axis=1)) - 1

def one_doc(doc_lengths, position):
    return doc_index(doc_lengths, jnp.reshape(position, (1,)).astype(jnp.int32))[0]

def settle(array):
    return lax.optimization_barrier(array.astype(jnp.bfloat16)).astype(jnp.float32)

def reference(queries, keys, values, gain, doc_lengths, cotangent):
    tile = TOK_DEV
    count = SEQ // tile
    reach = SPAN * tile
    scale = DH ** (-0.5)
    features = HEADS * DH
    offsets = jnp.arange(tile, dtype=jnp.int32)
    spread = jnp.arange(reach + tile, dtype=jnp.int32)
    causal = (offsets[:, None] >= offsets[None, :]).astype(jnp.float32)
    indices = jnp.arange(count, dtype=jnp.int32)
    zero_state = jnp.zeros((HEADS, DH, DH), jnp.float32)
    front = jnp.zeros((reach, HEADS, DH), jnp.bfloat16)
    key_pad = jnp.concatenate([front, keys], axis=0)
    value_pad = jnp.concatenate([front, values], axis=0)
    query_pad = jnp.concatenate([queries, front], axis=0)
    grad_pad = jnp.concatenate([cotangent, front], axis=0)

    def rows(array, start, size):
        return lax.dynamic_slice_in_dim(array, start, size, 0).astype(jnp.float32)

    def back_mask(start):
        query_pos = start + offsets
        key_pos = start - reach + spread
        same = doc_index(doc_lengths, query_pos)[:, None] == doc_index(doc_lengths, key_pos)[None, :]
        return same & (key_pos[None, :] <= query_pos[:, None])

    def scores_of(query_block, key_block, mask):
        raw = wide('thd,uhd->htu', query_block, key_block) * scale
        return jnp.where(mask[None], raw, neg_large)

    def tile_info(start):
        tile_doc = doc_index(doc_lengths, start + offsets)
        same = (tile_doc[:, None] == tile_doc[None, :]).astype(jnp.float32) * causal
        prev_doc = one_doc(doc_lengths, start - 1)
        next_doc = one_doc(doc_lengths, start + tile)
        return (tile_doc, same, prev_doc, next_doc)

    def forward(state, index):
        start = index * tile
        query_tile = rows(queries, start, tile)
        key_tile = rows(keys, start, tile)
        value_tile = rows(values, start, tile)
        tile_doc, same, prev_doc, next_doc = tile_info(start)
        carried = (tile_doc == prev_doc).astype(jnp.float32)
        attend = settle(wide('thd,uhd->htu', query_tile, key_tile) * same)
        linear_tile = wide('htu,uhd->thd', attend, value_tile) + wide('thd,hde->the', query_tile, state) * carried[:, None, None]
        scores = scores_of(query_tile, rows(key_pad, start, reach + tile), back_mask(start))
        top = lax.optimization_barrier(jnp.max(scores, axis=-1))
        log_total = top + jnp.log(lax.optimization_barrier(jnp.sum(jnp.exp(scores - top[..., None]), axis=-1)))
        weights = settle(jnp.exp(scores - log_total[..., None]))
        soft_tile = wide('htu,uhd->thd', weights, rows(value_pad, start, reach + tile))
        keep = (tile_doc == tile_doc[tile - 1]).astype(jnp.float32)
        stay = (prev_doc == tile_doc[tile - 1]).astype(jnp.float32)
        new_state = state * stay + wide('uhd,uhe->hde', key_tile * keep[:, None, None], value_tile)
        return (new_state, (linear_tile, soft_tile, log_total))
    final, (linear_out, soft_out, log_total) = lax.scan(forward, zero_state, indices)
    linear_out = linear_out.reshape(SEQ, HEADS, DH)
    soft_out = soft_out.reshape(SEQ, HEADS, DH)
    inverse = lax.rsqrt(lax.optimization_barrier(jnp.sum(linear_out * linear_out, axis=(1, 2))) / features + norm_eps)
    gain_wide = gain.astype(jnp.float32)
    mixed = (linear_out * inverse[:, None, None] * gain_wide[None] + soft_out).astype(jnp.bfloat16)
    grad = cotangent.astype(jnp.float32)
    weighted = grad * gain_wide[None]
    projection = lax.optimization_barrier(jnp.sum(weighted * linear_out, axis=(1, 2)))
    inner = settle(inverse[:, None, None] * weighted - linear_out * (inverse ** 3 * projection / features)[:, None, None])
    row_dot = lax.optimization_barrier(jnp.sum(grad * soft_out, axis=-1))
    dot_tiles = jnp.transpose(row_dot.reshape(count, tile, HEADS), (0, 2, 1))

    def query_side(state, inputs):
        index, lse_tile, dot_tile = inputs
        start = index * tile
        query_tile = rows(queries, start, tile)
        key_tile = rows(keys, start, tile)
        value_tile = rows(values, start, tile)
        inner_tile = lax.dynamic_slice_in_dim(inner, start, tile, 0)
        grad_tile = rows(cotangent, start, tile)
        key_window = rows(key_pad, start, reach + tile)
        value_window = rows(value_pad, start, reach + tile)
        tile_doc, same, prev_doc, next_doc = tile_info(start)
        carried = (tile_doc == prev_doc).astype(jnp.float32)
        back = settle(wide('thd,uhd->htu', inner_tile, value_tile) * same)
        linear_grad = wide('htu,uhd->thd', back, key_tile) + wide('the,hde->thd', inner_tile, state) * carried[:, None, None]
        scores = scores_of(query_tile, key_window, back_mask(start))
        probs = jnp.exp(scores - lse_tile[..., None])
        dprobs = wide('thd,uhd->htu', grad_tile, value_window)
        dscores = settle(probs * (dprobs - dot_tile[..., None]))
        soft_grad = wide('htu,uhd->thd', dscores, key_window) * scale
        keep = (tile_doc == tile_doc[tile - 1]).astype(jnp.float32)
        stay = (prev_doc == tile_doc[tile - 1]).astype(jnp.float32)
        new_state = state * stay + wide('uhd,uhe->hde', key_tile * keep[:, None, None], value_tile)
        return (new_state, linear_grad + soft_grad)
    final, query_grad = lax.scan(query_side, zero_state, (indices, log_total, dot_tiles))
    query_grad = query_grad.reshape(SEQ, HEADS, DH).astype(jnp.bfloat16)
    tail = jnp.zeros((reach, HEADS), jnp.float32)
    lse_rows = jnp.transpose(log_total, (0, 2, 1)).reshape(SEQ, HEADS)
    lse_pad = jnp.concatenate([lse_rows, tail], axis=0)
    dot_pad = jnp.concatenate([row_dot, tail], axis=0)

    def key_side(later, index):
        start = index * tile
        query_tile = rows(queries, start, tile)
        key_tile = rows(keys, start, tile)
        value_tile = rows(values, start, tile)
        inner_tile = lax.dynamic_slice_in_dim(inner, start, tile, 0)
        tile_doc, same, prev_doc, next_doc = tile_info(start)
        carried = (tile_doc == next_doc).astype(jnp.float32)
        attend = settle(wide('thd,uhd->htu', query_tile, key_tile) * same)
        back = settle(wide('thd,uhd->htu', inner_tile, value_tile) * same)
        key_linear = wide('htu,thd->uhd', back, query_tile) + wide('uhe,hde->uhd', value_tile, later) * carried[:, None, None]
        value_linear = wide('htu,the->uhe', attend, inner_tile) + wide('uhd,hde->uhe', key_tile, later) * carried[:, None, None]
        query_pos = start + spread
        key_pos = start + offsets
        same_doc = doc_index(doc_lengths, query_pos)[:, None] == doc_index(doc_lengths, key_pos)[None, :]
        mask = same_doc & (key_pos[None, :] <= query_pos[:, None]) & (query_pos[:, None] < SEQ)
        query_window = rows(query_pad, start, reach + tile)
        grad_window = rows(grad_pad, start, reach + tile)
        lse_window = lax.dynamic_slice_in_dim(lse_pad, start, reach + tile, 0).T
        dot_window = lax.dynamic_slice_in_dim(dot_pad, start, reach + tile, 0).T
        scores = scores_of(query_window, key_tile, mask)
        probs = jnp.exp(scores - lse_window[..., None])
        weights = settle(probs)
        dprobs = wide('thd,uhd->htu', grad_window, value_tile)
        dscores = settle(probs * (dprobs - dot_window[..., None]))
        key_soft = wide('htu,thd->uhd', dscores, query_window) * scale
        value_soft = wide('htu,thd->uhd', weights, grad_window)
        keep = (tile_doc == tile_doc[0]).astype(jnp.float32)
        stay = (next_doc == tile_doc[0]).astype(jnp.float32)
        new_later = later * stay + wide('thd,the->hde', query_tile * keep[:, None, None], inner_tile)
        return (new_later, (key_linear + key_soft, value_linear + value_soft))
    final, (key_grad, value_grad) = lax.scan(key_side, zero_state, indices, reverse=True)
    key_grad = key_grad.reshape(SEQ, HEADS, DH).astype(jnp.bfloat16)
    value_grad = value_grad.reshape(SEQ, HEADS, DH).astype(jnp.bfloat16)
    return (mixed, query_grad, key_grad, value_grad)
```

```python
import functools

import jax
import jax.numpy as jnp
from jax import lax
from jax.experimental import pallas as pl
from jax.experimental.pallas import tpu as pltpu
from jax.sharding import PartitionSpec as P

SPAN = 2


neg_large = -1e30
norm_eps = 1e-06


def from_behind(x, axis, by):
    devices = lax.axis_size(axis)
    pairs = [(i, i + by) for i in range(devices) if 0 <= i + by < devices]
    return lax.ppermute(x, axis, pairs)


def carried_in(part, axis, combine, reverse):
    count = lax.axis_size(axis)
    sign = -1 if reverse else 1

    def moved(part, by):
        return jax.tree.map(lambda a: from_behind(a, axis, sign * by), part)

    state, by = moved(part, 1), 1
    while by < count:
        state = combine(moved(state, by), state)
        by *= 2
    return state


def over_heads(x):
    groups = lax.axis_size("head")
    total = x
    for by in range(1, groups):
        pairs = [(i, (i + by) % groups) for i in range(groups)]
        total = total + lax.ppermute(x, "head", pairs)
    return total


def wide(form, left, right):
    return jnp.einsum(form, left, right, precision=lax.Precision.HIGHEST)


def narrow(form, left, right):
    return jnp.einsum(form, left, right, preferred_element_type=jnp.float32)


def doc_index(doc_lengths, positions):
    order = jnp.arange(doc_lengths.shape[0])
    starts = jnp.sum(jnp.where(order[None, :] < order[:, None], doc_lengths[None, :], 0), axis=1)
    return jnp.sum((starts[None, :] <= positions[:, None]).astype(jnp.int32), axis=1) - 1


def one_doc(doc_lengths, position):
    return doc_index(doc_lengths, jnp.reshape(position, (1,)))[0]


def join_states(earlier, later):
    return (later[0] + (1.0 - later[1]) * earlier[0], jnp.maximum(earlier[1], later[1]))


def masked_scores(query_block, key_block, mask, scale):
    raw = narrow("thd,uhd->htu", query_block, key_block) * scale
    return jnp.where(mask[None], raw, neg_large)


def key_terms(dscores, weights, query_block, grad_block, scale):
    key_part = narrow("htu,thd->uhd", dscores, query_block) * scale
    value_part = narrow("htu,thd->uhd", weights, grad_block)
    return (key_part, value_part)


def per_device(queries, keys, values, gain, doc_lengths, cotangent):
    tile, heads, width = queries.shape
    features = heads * lax.axis_size("head") * width
    scale = width ** (-0.5)
    base = lax.axis_index("ctx") * tile
    offsets = jnp.arange(tile, dtype=jnp.int32)
    own_pos = base + offsets
    own_doc = doc_index(doc_lengths, own_pos)
    prev_doc = one_doc(doc_lengths, base - 1)
    next_doc = one_doc(doc_lengths, base + tile)
    pair = jnp.stack([keys, values])
    arrived = [from_behind(pair, "ctx", shift) for shift in range(SPAN, 0, -1)]
    key_tiles = [piece[0] for piece in arrived] + [keys]
    value_tiles = [piece[1] for piece in arrived] + [values]
    masks = []
    for position in range(SPAN + 1):
        key_pos = base - (SPAN - position) * tile + offsets
        key_doc = doc_index(doc_lengths, key_pos)
        masks.append(
            (own_doc[:, None] == key_doc[None, :]) & (key_pos[None, :] <= own_pos[:, None])
        )
    score_list = [
        masked_scores(queries, key_tiles[position], masks[position], scale)
        for position in range(SPAN + 1)
    ]
    top = score_list[0].max(axis=-1)
    for position in range(1, SPAN + 1):
        top = jnp.maximum(top, score_list[position].max(axis=-1))
    total = jnp.zeros((heads, tile), jnp.float32)
    for position in range(SPAN + 1):
        total = total + jnp.sum(jnp.exp(score_list[position] - top[..., None]), axis=-1)
    log_total = top + jnp.log(total)
    prob_list = []
    weight_list = []
    soft_out = jnp.zeros((tile, heads, width), jnp.float32)
    for position in range(SPAN + 1):
        probs = jnp.exp(score_list[position] - log_total[..., None])
        weights = probs.astype(jnp.bfloat16)
        prob_list.append(probs)
        weight_list.append(weights)
        soft_out = soft_out + narrow("htu,uhd->thd", weights, value_tiles[position])
    same_tile = masks[SPAN].astype(jnp.float32)
    carried_prev = (own_doc == prev_doc).astype(jnp.float32)
    carried_next = (own_doc == next_doc).astype(jnp.float32)
    keep_last = (own_doc == own_doc[tile - 1])[:, None, None]
    keep_first = (own_doc == own_doc[0])[:, None, None]
    reset_front = (prev_doc != own_doc[tile - 1]).astype(jnp.float32)
    reset_back = (next_doc != own_doc[0]).astype(jnp.float32)
    query_wide = queries.astype(jnp.float32)
    attend = (narrow("thd,uhd->htu", queries, keys) * same_tile).astype(jnp.bfloat16)
    local_state = narrow("uhd,uhe->hde", jnp.where(keep_last, keys, jnp.zeros_like(keys)), values)
    incoming, front_flag = carried_in(
        (local_state, reset_front), "ctx", join_states, False
    )
    linear_out = (
        narrow("htu,uhd->thd", attend, values)
        + wide("thd,hde->the", query_wide, incoming) * carried_prev[:, None, None]
    )
    squares = over_heads(jnp.sum(linear_out * linear_out, axis=(1, 2)))
    inverse = lax.rsqrt(squares / features + norm_eps)
    mixed = (linear_out * inverse[:, None, None] * gain[None] + soft_out).astype(jnp.bfloat16)
    grad_wide = cotangent.astype(jnp.float32)
    weighted = grad_wide * gain[None]
    projection = over_heads(jnp.sum(weighted * linear_out, axis=(1, 2)))
    inner = (
        inverse[:, None, None] * weighted
        - linear_out * (inverse**3 * projection / features)[:, None, None]
    ).astype(jnp.bfloat16)
    row_dot = jnp.sum(grad_wide * soft_out, axis=-1).T
    query_soft = jnp.zeros((tile, heads, width), jnp.float32)
    dscore_list = []
    for position in range(SPAN + 1):
        dprobs = narrow("thd,uhd->htu", cotangent, value_tiles[position])
        dscores = (prob_list[position] * (dprobs - row_dot[..., None])).astype(jnp.bfloat16)
        query_soft = query_soft + narrow("htu,uhd->thd", dscores, key_tiles[position]) * scale
        dscore_list.append(dscores)
    inner_wide = inner.astype(jnp.float32)
    back = (narrow("thd,uhd->htu", inner, values) * same_tile).astype(jnp.bfloat16)
    query_linear = (
        narrow("htu,uhd->thd", back, keys)
        + wide("the,hde->thd", inner_wide, incoming) * carried_prev[:, None, None]
    )
    tile_sum = narrow(
        "thd,the->hde", jnp.where(keep_first, queries, jnp.zeros_like(queries)), inner
    )
    later, back_flag = carried_in(
        (tile_sum, reset_back), "ctx", join_states, True
    )
    key_linear = (
        narrow("htu,thd->uhd", back, queries)
        + wide("uhe,hde->uhd", values.astype(jnp.float32), later) * carried_next[:, None, None]
    )
    value_linear = (
        narrow("htu,the->uhe", attend, inner)
        + wide("uhd,hde->uhe", keys.astype(jnp.float32), later) * carried_next[:, None, None]
    )
    parts = [
        key_terms(dscore_list[position], weight_list[position], queries, cotangent, scale)
        for position in range(SPAN + 1)
    ]
    key_soft, value_soft = parts[SPAN]
    for shift in range(1, SPAN + 1):
        sent = jnp.stack([parts[SPAN - shift][0], parts[SPAN - shift][1]])
        returned = from_behind(sent.astype(jnp.bfloat16), "ctx", -shift).astype(sent.dtype)
        key_soft = key_soft + returned[0]
        value_soft = value_soft + returned[1]
    query_grad = (query_linear + query_soft).astype(jnp.bfloat16)
    key_grad = (key_linear + key_soft).astype(jnp.bfloat16)
    value_grad = (value_linear + value_soft).astype(jnp.bfloat16)
    return (mixed, query_grad, key_grad, value_grad)


def mm(left, right, dims):
    return lax.dot_general(left, right, (dims, ((), ())), preferred_element_type=jnp.float32)


NT = ((1,), (1,))
NN = ((1,), (0,))
TN = ((0,), (0,))


def block_kernel(
    count, groups, features,
    len_ref, q_ref, k_ref, v_ref, g_ref, do_ref,
    mixed_ref, qg_ref, kg_ref, vg_ref,
    wide_a, wide_b, q_own, qm_own, do_own, win, bias, keep, attend, lin, soft,
    dq, dkv, part2, part1_tx, part2_tx, rx1, rx2, inner, t_tx, tx1, tz,
    sq_acc, pj_acc, inv_b, coef_b, stat_tx, stat_rx,
    kvz_s, kvz_r, kvx_s, kvx_r, pz_s, pz_r, px_s, px_r, tz_s, tz_r, tx_s, tx_r, st_s, st_r,
):
    heads, tile, width = q_own.shape
    scale = width ** (-0.5)
    bf = jnp.bfloat16
    f32 = jnp.float32
    me = lax.axis_index("ctx")
    group = lax.axis_index("head")
    odd = lax.rem(me, 2) == 1
    even = lax.rem(me, 2) == 0
    has_prev = me >= 2
    has_next = me < count - 2
    side = me + 1 - 2 * lax.rem(me, 2)

    def remote(src, dst, send, recv, axis, to):
        return pltpu.make_async_remote_copy(
            src_ref=src, dst_ref=dst, send_sem=send, recv_sem=recv,
            device_id={axis: to}, device_id_type=pl.DeviceIdType.MESH,
        )

    old, mid, own = pl.ds(0, tile), pl.ds(tile, tile), pl.ds(2 * tile, tile)

    def kv_z(h):
        return remote(win.at[h, :, own], win.at[h, :, old], kvz_s.at[h], kvz_r.at[h], "ctx", me + 2)

    def kv_x_own(h):
        return remote(win.at[h, :, own], win.at[h, :, mid], kvx_s.at[h], kvx_r.at[h], "ctx", side)

    def kv_x_relay(h):
        return remote(win.at[h, :, old], win.at[h, :, mid], kvx_s.at[h], kvx_r.at[h], "ctx", side)

    def part_x(h):
        return remote(part1_tx.at[h], rx1.at[h], px_s.at[h], px_r.at[h], "ctx", side)

    def part_z(h):
        return remote(part2_tx.at[h], rx2.at[h], pz_s.at[h], pz_r.at[h], "ctx", me - 2)

    def state_z(h):
        return remote(t_tx.at[h], tz.at[h], tz_s.at[h], tz_r.at[h], "ctx", me - 2)

    def state_x_own(h):
        return remote(t_tx.at[h], tx1.at[h], tx_s.at[h], tx_r.at[h], "ctx", side)

    def state_x_relay(h):
        return remote(tz.at[h], tx1.at[h], tx_s.at[h], tx_r.at[h], "ctx", side)

    def stats(k):
        return remote(
            stat_tx, stat_rx.at[k - 1], st_s.at[k - 1], st_r.at[k - 1], "head",
            lax.rem(group + k, groups),
        )

    def greet(axis, to):
        pl.semaphore_signal(
            barrier, inc=1, device_id={axis: to}, device_id_type=pl.DeviceIdType.MESH
        )

    barrier = pltpu.get_barrier_semaphore()
    greet("ctx", side)
    for k in range(1, groups):
        greet("head", lax.rem(group + k, groups))

    @pl.when(has_prev)
    def _():
        greet("ctx", me - 2)

    @pl.when(has_next)
    def _():
        greet("ctx", me + 2)

    wide_a[...] = k_ref[...].astype(f32).reshape(tile * heads, width)
    wide_b[...] = v_ref[...].astype(f32).reshape(tile * heads, width)
    for h in range(heads):
        win[h, 0, 2 * tile:3 * tile, :] = wide_a[pl.ds(h, tile, stride=heads), :].astype(bf)
        win[h, 1, 2 * tile:3 * tile, :] = wide_b[pl.ds(h, tile, stride=heads), :].astype(bf)

    pl.semaphore_wait(barrier, groups + has_prev.astype(jnp.int32) + has_next.astype(jnp.int32))

    def send_kv(h, carry):
        @pl.when(has_next)
        def _():
            kv_z(h).start()

        @pl.when(even)
        def _():
            kv_x_own(h).start()

        return carry

    lax.fori_loop(0, heads, send_kv, 0)

    starts = []
    running = jnp.int32(0)
    for d in range(len_ref.shape[0]):
        starts.append(running)
        running = running + len_ref[d]
    base = me * tile

    def doc_of(position):
        total = jnp.zeros_like(position)
        for start in starts:
            total = total + jnp.where(position >= start, 1, 0).astype(jnp.int32)
        return total

    rows = lax.broadcasted_iota(jnp.int32, (tile, tile), 0)
    cols = lax.broadcasted_iota(jnp.int32, (tile, tile), 1)
    own_pos = base + rows
    own_doc = doc_of(own_pos)
    for position in range(3):
        key_pos = base - (2 - position) * tile + cols
        allowed = (own_doc == doc_of(key_pos)) & (key_pos <= own_pos)
        place = slice(position * tile, (position + 1) * tile)
        bias[:, place] = jnp.where(allowed, 0.0, neg_large).astype(f32)
        keep[:, place] = jnp.where(allowed, 1.0, 0.0).astype(f32)
    first_doc = doc_of(base)
    next_doc = doc_of(base + tile)
    after_doc = doc_of(base + 2 * tile)
    in_first = jnp.where(own_doc == first_doc, 1.0, 0.0).astype(f32)
    in_next = jnp.where(own_doc == next_doc, 1.0, 0.0).astype(f32)
    join = jnp.where(next_doc == after_doc, 1.0, 0.0).astype(f32)
    is_even = jnp.where(even, 1.0, 0.0).astype(f32)

    wide_a[...] = q_ref[...].astype(f32).reshape(tile * heads, width)
    wide_b[...] = do_ref[...].astype(f32).reshape(tile * heads, width)
    for h in range(heads):
        q_h = wide_a[pl.ds(h, tile, stride=heads), :]
        q_own[h] = q_h.astype(bf)
        qm_own[h] = (q_h * in_first).astype(bf)
        do_own[h] = wide_b[pl.ds(h, tile, stride=heads), :].astype(bf)
    sq_acc[...] = jnp.zeros_like(sq_acc)
    pj_acc[...] = jnp.zeros_like(pj_acc)

    @pl.when(me < 2)
    def _():
        win[:, :, 0:tile, :] = jnp.zeros((heads, 2, tile, width), bf)

    @pl.when(me == 0)
    def _():
        win[:, :, tile:2 * tile, :] = jnp.zeros((heads, 2, tile, width), bf)

    @pl.when(me == 1)
    def _():
        rx1[...] = jnp.zeros_like(rx1)

    @pl.when(me >= count - 2)
    def _():
        rx2[...] = jnp.zeros_like(rx2)
        tz[...] = jnp.zeros_like(tz)

    @pl.when(me == count - 1)
    def _():
        tx1[...] = jnp.zeros_like(tx1)

    def pass_on(h):
        part_x(h).wait_recv()
        part2_tx[h] = (part2[h] + rx1[h].astype(f32)).astype(bf)
        part_z(h).start()

    def soft_step(h, carry):
        @pl.when(has_prev)
        def _():
            kv_z(h).wait_recv()

        @pl.when(odd & has_prev)
        def _():
            kv_x_relay(h).start()

        @pl.when(odd | has_prev)
        def _():
            kv_x_own(h).wait_recv()

        q_h, do_h = q_own[h], do_own[h]
        k_w, v_w = win[h, 0], win[h, 1]
        raw = mm(q_h, k_w, NT)
        scores = raw * scale + bias[...]
        top = jnp.max(scores, axis=-1, keepdims=True)
        grown = jnp.exp(scores - top)
        probs = grown * (1.0 / jnp.sum(grown, axis=-1, keepdims=True))
        weights = probs.astype(bf)
        soft_h = mm(weights, v_w, NN)
        att = (raw * keep[...]).astype(bf)
        lin_h = mm(att, v_w, NN)
        grad = do_h.astype(f32)
        row_dot = jnp.sum(grad * soft_h, axis=-1, keepdims=True)
        dscores = (probs * (mm(do_h, v_w, NT) - row_dot)).astype(bf)
        dq[h] = mm(dscores, k_w, NN) * scale
        dk_w = mm(dscores, q_h, TN) * scale
        dv_w = mm(weights, do_h, TN)
        lin[h] = lin_h
        soft[h] = soft_h
        attend[h] = att[:, 2 * tile:]
        dkv[h, 0] = dk_w[2 * tile:]
        dkv[h, 1] = dv_w[2 * tile:]
        part1_tx[h, 0] = dk_w[tile:2 * tile].astype(bf)
        part1_tx[h, 1] = dv_w[tile:2 * tile].astype(bf)
        sq_acc[...] += lin_h * lin_h
        pj_acc[...] += grad * g_ref[pl.ds(h, 1), :] * lin_h

        @pl.when(odd | has_prev)
        def _():
            part_x(h).start()

        @pl.when(even & has_prev)
        def _():
            part2_tx[h, 0] = dk_w[:tile].astype(bf)
            part2_tx[h, 1] = dv_w[:tile].astype(bf)
            part_z(h).start()

        @pl.when(odd & has_prev)
        def _():
            part2[h, 0] = dk_w[:tile]
            part2[h, 1] = dv_w[:tile]

        @pl.when(odd & has_prev & (h >= 2))
        def _():
            pass_on(jnp.maximum(h - 2, 0))

        return carry

    lax.fori_loop(0, heads, soft_step, 0)

    sq_col = jnp.sum(sq_acc[...], axis=-1, keepdims=True)
    pj_col = jnp.sum(pj_acc[...], axis=-1, keepdims=True)
    flat = jnp.where(cols == 0, sq_col, jnp.where(cols == 1, pj_col, 0.0)).T
    stat_tx[...] = flat[:8]
    for k in range(1, groups):
        stats(k).start()

    @pl.when(odd & has_prev)
    def _():
        lax.fori_loop(heads - 2, heads, lambda h, c: (pass_on(h), c)[1], 0)

    total = stat_tx[...]
    for k in range(1, groups):
        stats(k).wait_recv()
        total = total + stat_rx[k - 1]
    back_flat = jnp.concatenate([total, jnp.zeros((tile - 8, tile), f32)], axis=0).T
    sq_sum = back_flat[:, 0:1]
    pj_sum = back_flat[:, 1:2]
    inverse = lax.rsqrt(sq_sum / features + norm_eps)
    inv_b[...] = jnp.broadcast_to(inverse, (tile, width))
    coef_b[...] = jnp.broadcast_to(inverse * inverse * inverse * pj_sum / features, (tile, width))

    def state_step(h, carry):
        weighted = do_own[h].astype(f32) * g_ref[pl.ds(h, 1), :]
        inner_h = (inv_b[...] * weighted - lin[h] * coef_b[...]).astype(bf)
        inner[h] = inner_h
        t_tx[h] = mm(qm_own[h], inner_h, TN).astype(bf)

        @pl.when(has_prev)
        def _():
            state_z(h).start()

        @pl.when(odd)
        def _():
            state_x_own(h).start()

        return carry

    lax.fori_loop(0, heads, state_step, 0)

    def local_step(h, carry):
        @pl.when(has_next)
        def _():
            state_z(h).wait_recv()

        @pl.when(even & has_next)
        def _():
            state_x_relay(h).start()

        inner_h = inner[h]
        back = (mm(inner_h, win[h, 1], NT) * keep[...]).astype(bf)
        dq[h] += mm(back, win[h, 0], NN)
        dkv[h, 0] += mm(back[:, 2 * tile:], q_own[h], TN)
        dkv[h, 1] += mm(attend[h], inner_h, TN)
        soft[h] += lin[h] * inv_b[...] * g_ref[pl.ds(h, 1), :]
        return carry

    lax.fori_loop(0, heads, local_step, 0)

    for h in range(heads):
        wide_a[pl.ds(h, tile, stride=heads), :] = soft[h]
        wide_b[pl.ds(h, tile, stride=heads), :] = dq[h]
    mixed_ref[...] = wide_a[...].reshape(tile, heads, width).astype(bf)
    qg_ref[...] = wide_b[...].reshape(tile, heads, width).astype(bf)

    def last_step(h, carry):
        @pl.when(has_next)
        def _():
            part_z(h).wait_recv()

        @pl.when(even)
        def _():
            part_x(h).wait_recv()

        @pl.when(even | has_next)
        def _():
            state_x_own(h).wait_recv()

        state = (tx1[h].astype(f32) + join * tz[h].astype(f32)).astype(bf)
        got = rx1[h].astype(f32) * is_even + rx2[h].astype(f32)
        dkv[h, 0] += got[0] + in_next * mm(win[h, 1, own, :], state, NT)
        dkv[h, 1] += got[1] + in_next * mm(win[h, 0, own, :], state, NN)
        return carry

    lax.fori_loop(0, heads, last_step, 0)

    for h in range(heads):
        wide_a[pl.ds(h, tile, stride=heads), :] = dkv[h, 0]
        wide_b[pl.ds(h, tile, stride=heads), :] = dkv[h, 1]
    kg_ref[...] = wide_a[...].reshape(tile, heads, width).astype(bf)
    vg_ref[...] = wide_b[...].reshape(tile, heads, width).astype(bf)

    def drain(h, carry):
        @pl.when(has_next)
        def _():
            kv_z(h).wait_send()

        @pl.when(even | has_prev)
        def _():
            kv_x_own(h).wait_send()

        @pl.when(odd | has_prev)
        def _():
            part_x(h).wait_send()

        @pl.when(has_prev)
        def _():
            part_z(h).wait_send()
            state_z(h).wait_send()

        @pl.when(odd | has_next)
        def _():
            state_x_own(h).wait_send()

        return carry

    lax.fori_loop(0, heads, drain, 0)
    for k in range(1, groups):
        stats(k).wait_send()


def in_window(queries, keys, values, gain, doc_lengths, cotangent):
    tile, heads, width = queries.shape
    count, groups = lax.axis_size("ctx"), lax.axis_size("head")
    bf, f32 = jnp.bfloat16, jnp.float32
    block = (heads, tile, width)
    pair = (heads, 2, tile, width)
    vmem = pl.BlockSpec(memory_space=pltpu.VMEM)
    each = pltpu.SemaphoreType.DMA((heads,))
    return pl.pallas_call(
        functools.partial(block_kernel, count, groups, heads * groups * width),
        out_shape=[jax.ShapeDtypeStruct(queries.shape, bf)] * 4,
        in_specs=[pl.BlockSpec(memory_space=pltpu.SMEM)] + [vmem] * 5,
        out_specs=[vmem] * 4,
        scratch_shapes=[
            pltpu.VMEM((tile * heads, width), f32),
            pltpu.VMEM((tile * heads, width), f32),
            pltpu.VMEM(block, bf),
            pltpu.VMEM(block, bf),
            pltpu.VMEM(block, bf),
            pltpu.VMEM((heads, 2, 3 * tile, width), bf),
            pltpu.VMEM((tile, 3 * tile), f32),
            pltpu.VMEM((tile, 3 * tile), f32),
            pltpu.VMEM((heads, tile, tile), bf),
            pltpu.VMEM(block, f32),
            pltpu.VMEM(block, f32),
            pltpu.VMEM(block, f32),
            pltpu.VMEM(pair, f32),
            pltpu.VMEM(pair, f32),
            pltpu.VMEM(pair, bf),
            pltpu.VMEM(pair, bf),
            pltpu.VMEM(pair, bf),
            pltpu.VMEM(pair, bf),
            pltpu.VMEM(block, bf),
            pltpu.VMEM((heads, width, width), bf),
            pltpu.VMEM((heads, width, width), bf),
            pltpu.VMEM((heads, width, width), bf),
            pltpu.VMEM((tile, width), f32),
            pltpu.VMEM((tile, width), f32),
            pltpu.VMEM((tile, width), f32),
            pltpu.VMEM((tile, width), f32),
            pltpu.VMEM((8, tile), f32),
            pltpu.VMEM((groups - 1, 8, tile), f32),
        ]
        + [each] * 12
        + [pltpu.SemaphoreType.DMA((groups - 1,))] * 2,
        compiler_params=pltpu.CompilerParams(
            collective_id=0, has_side_effects=True, vmem_limit_bytes=40 * 1024 * 1024
        ),
    )(doc_lengths, queries, keys, values, gain, cotangent)


def dispatch(queries, keys, values, gain, doc_lengths, cotangent):
    tile = queries.shape[0]
    count = lax.axis_size("ctx")
    if count * tile <= 4 * SPAN * tile and count % 2 == 0:
        return tuple(in_window(queries, keys, values, gain, doc_lengths, cotangent))
    return per_device(queries, keys, values, gain, doc_lengths, cotangent)


def solution(mesh):
    placed = (
        P("ctx", "head", None),
        P("ctx", "head", None),
        P("ctx", "head", None),
        P("head", None),
        P(),
        P("ctx", "head", None),
    )
    return jax.shard_map(
        dispatch,
        mesh=mesh,
        in_specs=placed,
        out_specs=(
            P("ctx", "head", None),
            P("ctx", "head", None),
            P("ctx", "head", None),
            P("ctx", "head", None),
        ),
        check_vma=False,
    )
```

```python
import functools

import jax
import jax.numpy as jnp
from jax import lax
from jax.experimental import pallas as pl
from jax.experimental.pallas import tpu as pltpu
from jax.sharding import PartitionSpec as P

SPAN = 2


neg_large = -1e30
norm_eps = 1e-06


def from_behind(x, axis, by):
    devices = lax.axis_size(axis)
    pairs = [(i, i + by) for i in range(devices) if 0 <= i + by < devices]
    return lax.ppermute(x, axis, pairs)


def carried_in(part, axis, combine, reverse):
    count = lax.axis_size(axis)
    sign = -1 if reverse else 1

    def moved(part, by):
        return jax.tree.map(lambda a: from_behind(a, axis, sign * by), part)

    state, by = moved(part, 1), 1
    while by < count:
        state = combine(moved(state, by), state)
        by *= 2
    return state


def over_heads(x):
    groups = lax.axis_size("head")
    total = x
    for by in range(1, groups):
        pairs = [(i, (i + by) % groups) for i in range(groups)]
        total = total + lax.ppermute(x, "head", pairs)
    return total


def wide(form, left, right):
    return jnp.einsum(form, left, right, precision=lax.Precision.HIGHEST)


def narrow(form, left, right):
    return jnp.einsum(form, left, right, preferred_element_type=jnp.float32)


def doc_index(doc_lengths, positions):
    order = jnp.arange(doc_lengths.shape[0])
    starts = jnp.sum(jnp.where(order[None, :] < order[:, None], doc_lengths[None, :], 0), axis=1)
    return jnp.sum((starts[None, :] <= positions[:, None]).astype(jnp.int32), axis=1) - 1


def one_doc(doc_lengths, position):
    return doc_index(doc_lengths, jnp.reshape(position, (1,)))[0]


def join_states(earlier, later):
    return (later[0] + (1.0 - later[1]) * earlier[0], jnp.maximum(earlier[1], later[1]))


def masked_scores(query_block, key_block, mask, scale):
    raw = narrow("thd,uhd->htu", query_block, key_block) * scale
    return jnp.where(mask[None], raw, neg_large)


def key_terms(dscores, weights, query_block, grad_block, scale):
    key_part = narrow("htu,thd->uhd", dscores, query_block) * scale
    value_part = narrow("htu,thd->uhd", weights, grad_block)
    return (key_part, value_part)


def per_device(queries, keys, values, gain, doc_lengths, cotangent):
    tile, heads, width = queries.shape
    features = heads * lax.axis_size("head") * width
    scale = width ** (-0.5)
    base = lax.axis_index("ctx") * tile
    offsets = jnp.arange(tile, dtype=jnp.int32)
    own_pos = base + offsets
    own_doc = doc_index(doc_lengths, own_pos)
    prev_doc = one_doc(doc_lengths, base - 1)
    next_doc = one_doc(doc_lengths, base + tile)
    pair = jnp.stack([keys, values])
    arrived = [from_behind(pair, "ctx", shift) for shift in range(SPAN, 0, -1)]
    key_tiles = [piece[0] for piece in arrived] + [keys]
    value_tiles = [piece[1] for piece in arrived] + [values]
    masks = []
    for position in range(SPAN + 1):
        key_pos = base - (SPAN - position) * tile + offsets
        key_doc = doc_index(doc_lengths, key_pos)
        masks.append(
            (own_doc[:, None] == key_doc[None, :]) & (key_pos[None, :] <= own_pos[:, None])
        )
    score_list = [
        masked_scores(queries, key_tiles[position], masks[position], scale)
        for position in range(SPAN + 1)
    ]
    top = score_list[0].max(axis=-1)
    for position in range(1, SPAN + 1):
        top = jnp.maximum(top, score_list[position].max(axis=-1))
    total = jnp.zeros((heads, tile), jnp.float32)
    for position in range(SPAN + 1):
        total = total + jnp.sum(jnp.exp(score_list[position] - top[..., None]), axis=-1)
    log_total = top + jnp.log(total)
    prob_list = []
    weight_list = []
    soft_out = jnp.zeros((tile, heads, width), jnp.float32)
    for position in range(SPAN + 1):
        probs = jnp.exp(score_list[position] - log_total[..., None])
        weights = probs.astype(jnp.bfloat16)
        prob_list.append(probs)
        weight_list.append(weights)
        soft_out = soft_out + narrow("htu,uhd->thd", weights, value_tiles[position])
    same_tile = masks[SPAN].astype(jnp.float32)
    carried_prev = (own_doc == prev_doc).astype(jnp.float32)
    carried_next = (own_doc == next_doc).astype(jnp.float32)
    keep_last = (own_doc == own_doc[tile - 1])[:, None, None]
    keep_first = (own_doc == own_doc[0])[:, None, None]
    reset_front = (prev_doc != own_doc[tile - 1]).astype(jnp.float32)
    reset_back = (next_doc != own_doc[0]).astype(jnp.float32)
    query_wide = queries.astype(jnp.float32)
    attend = (narrow("thd,uhd->htu", queries, keys) * same_tile).astype(jnp.bfloat16)
    local_state = narrow("uhd,uhe->hde", jnp.where(keep_last, keys, jnp.zeros_like(keys)), values)
    incoming, front_flag = carried_in(
        (local_state, reset_front), "ctx", join_states, False
    )
    linear_out = (
        narrow("htu,uhd->thd", attend, values)
        + wide("thd,hde->the", query_wide, incoming) * carried_prev[:, None, None]
    )
    squares = over_heads(jnp.sum(linear_out * linear_out, axis=(1, 2)))
    inverse = lax.rsqrt(squares / features + norm_eps)
    mixed = (linear_out * inverse[:, None, None] * gain[None] + soft_out).astype(jnp.bfloat16)
    grad_wide = cotangent.astype(jnp.float32)
    weighted = grad_wide * gain[None]
    projection = over_heads(jnp.sum(weighted * linear_out, axis=(1, 2)))
    inner = (
        inverse[:, None, None] * weighted
        - linear_out * (inverse**3 * projection / features)[:, None, None]
    ).astype(jnp.bfloat16)
    row_dot = jnp.sum(grad_wide * soft_out, axis=-1).T
    query_soft = jnp.zeros((tile, heads, width), jnp.float32)
    dscore_list = []
    for position in range(SPAN + 1):
        dprobs = narrow("thd,uhd->htu", cotangent, value_tiles[position])
        dscores = (prob_list[position] * (dprobs - row_dot[..., None])).astype(jnp.bfloat16)
        query_soft = query_soft + narrow("htu,uhd->thd", dscores, key_tiles[position]) * scale
        dscore_list.append(dscores)
    inner_wide = inner.astype(jnp.float32)
    back = (narrow("thd,uhd->htu", inner, values) * same_tile).astype(jnp.bfloat16)
    query_linear = (
        narrow("htu,uhd->thd", back, keys)
        + wide("the,hde->thd", inner_wide, incoming) * carried_prev[:, None, None]
    )
    tile_sum = narrow(
        "thd,the->hde", jnp.where(keep_first, queries, jnp.zeros_like(queries)), inner
    )
    later, back_flag = carried_in(
        (tile_sum, reset_back), "ctx", join_states, True
    )
    key_linear = (
        narrow("htu,thd->uhd", back, queries)
        + wide("uhe,hde->uhd", values.astype(jnp.float32), later) * carried_next[:, None, None]
    )
    value_linear = (
        narrow("htu,the->uhe", attend, inner)
        + wide("uhd,hde->uhe", keys.astype(jnp.float32), later) * carried_next[:, None, None]
    )
    parts = [
        key_terms(dscore_list[position], weight_list[position], queries, cotangent, scale)
        for position in range(SPAN + 1)
    ]
    key_soft, value_soft = parts[SPAN]
    for shift in range(1, SPAN + 1):
        sent = jnp.stack([parts[SPAN - shift][0], parts[SPAN - shift][1]])
        returned = from_behind(sent.astype(jnp.bfloat16), "ctx", -shift).astype(sent.dtype)
        key_soft = key_soft + returned[0]
        value_soft = value_soft + returned[1]
    query_grad = (query_linear + query_soft).astype(jnp.bfloat16)
    key_grad = (key_linear + key_soft).astype(jnp.bfloat16)
    value_grad = (value_linear + value_soft).astype(jnp.bfloat16)
    return (mixed, query_grad, key_grad, value_grad)


def mm(left, right, dims):
    return lax.dot_general(left, right, (dims, ((), ())), preferred_element_type=jnp.float32)


NT = ((1,), (1,))
NN = ((1,), (0,))
TN = ((0,), (0,))


def block_kernel(
    count, groups, features,
    len_ref, q_hbm, k_hbm, v_hbm, g_hbm, do_hbm,
    mixed_ref, qg_ref, kg_ref, vg_ref,
    q_ref, k_ref, v_ref, g_ref, do_ref, in_sem,
    wide_a, wide_b, q_own, qm_own, do_own, win, bias, keep, attend, lin, soft,
    dq, dkv, part2, part1_tx, part2_tx, rx1, rx2, inner, t_tx, tx1, tz,
    sq_acc, pj_acc, inv_b, coef_b, stat_tx, stat_rx,
    kvz_s, kvz_r, kvx_s, kvx_r, pz_s, pz_r, px_s, px_r, tz_s, tz_r, tx_s, tx_r, st_s, st_r,
):
    heads, tile, width = q_own.shape
    scale = width ** (-0.5)
    bf = jnp.bfloat16
    f32 = jnp.float32
    me = lax.axis_index("ctx")
    group = lax.axis_index("head")
    odd = lax.rem(me, 2) == 1
    even = lax.rem(me, 2) == 0
    has_prev = me >= 2
    has_next = me < count - 2
    side = me + 1 - 2 * lax.rem(me, 2)
    lag = heads // 2

    def remote(src, dst, send, recv, axis, to):
        return pltpu.make_async_remote_copy(
            src_ref=src, dst_ref=dst, send_sem=send, recv_sem=recv,
            device_id={axis: to}, device_id_type=pl.DeviceIdType.MESH,
        )

    old, mid, own = pl.ds(0, tile), pl.ds(tile, tile), pl.ds(2 * tile, tile)

    def kv_z(h):
        return remote(win.at[h, :, own], win.at[h, :, old], kvz_s.at[h], kvz_r.at[h], "ctx", me + 2)

    def kv_x_own(h):
        return remote(win.at[h, :, own], win.at[h, :, mid], kvx_s.at[h], kvx_r.at[h], "ctx", side)

    def kv_x_relay(h):
        return remote(win.at[h, :, old], win.at[h, :, mid], kvx_s.at[h], kvx_r.at[h], "ctx", side)

    def part_x(h):
        return remote(part1_tx.at[h], rx1.at[h], px_s.at[h], px_r.at[h], "ctx", side)

    def part_z(h):
        return remote(part2_tx.at[h], rx2.at[h], pz_s.at[h], pz_r.at[h], "ctx", me - 2)

    def state_z(h):
        return remote(t_tx.at[h], tz.at[h], tz_s.at[h], tz_r.at[h], "ctx", me - 2)

    def state_x_own(h):
        return remote(t_tx.at[h], tx1.at[h], tx_s.at[h], tx_r.at[h], "ctx", side)

    def state_x_relay(h):
        return remote(tz.at[h], tx1.at[h], tx_s.at[h], tx_r.at[h], "ctx", side)

    def stats(k):
        return remote(
            stat_tx, stat_rx.at[k - 1], st_s.at[k - 1], st_r.at[k - 1], "head",
            lax.rem(group + k, groups),
        )

    def greet(axis, to):
        pl.semaphore_signal(
            barrier, inc=1, device_id={axis: to}, device_id_type=pl.DeviceIdType.MESH
        )

    loads = [
        pltpu.make_async_copy(source, target, in_sem.at[n])
        for n, (source, target) in enumerate(
            [(k_hbm, k_ref), (v_hbm, v_ref), (q_hbm, q_ref), (do_hbm, do_ref), (g_hbm, g_ref)]
        )
    ]
    for load in loads:
        load.start()
    barrier = pltpu.get_barrier_semaphore()
    greet("ctx", side)
    for k in range(1, groups):
        greet("head", lax.rem(group + k, groups))

    @pl.when(has_prev)
    def _():
        greet("ctx", me - 2)

    @pl.when(has_next)
    def _():
        greet("ctx", me + 2)

    loads[0].wait()
    loads[1].wait()
    wide_a[...] = k_ref[...].astype(f32).reshape(tile * heads, width)
    wide_b[...] = v_ref[...].astype(f32).reshape(tile * heads, width)
    for h in range(heads):
        win[h, 0, 2 * tile:3 * tile, :] = wide_a[pl.ds(h, tile, stride=heads), :].astype(bf)
        win[h, 1, 2 * tile:3 * tile, :] = wide_b[pl.ds(h, tile, stride=heads), :].astype(bf)

    pl.semaphore_wait(barrier, groups + has_prev.astype(jnp.int32) + has_next.astype(jnp.int32))

    def send_kv(h, carry):
        @pl.when(has_next)
        def _():
            kv_z(h).start()

        @pl.when(even)
        def _():
            kv_x_own(h).start()

        return carry

    lax.fori_loop(0, heads, send_kv, 0)

    starts = []
    running = jnp.int32(0)
    for d in range(len_ref.shape[0]):
        starts.append(running)
        running = running + len_ref[d]
    base = me * tile

    def doc_of(position):
        total = jnp.zeros_like(position)
        for start in starts:
            total = total + jnp.where(position >= start, 1, 0).astype(jnp.int32)
        return total

    rows = lax.broadcasted_iota(jnp.int32, (tile, tile), 0)
    cols = lax.broadcasted_iota(jnp.int32, (tile, tile), 1)
    own_pos = base + rows
    own_doc = doc_of(own_pos)
    for position in range(3):
        key_pos = base - (2 - position) * tile + cols
        allowed = (own_doc == doc_of(key_pos)) & (key_pos <= own_pos)
        place = slice(position * tile, (position + 1) * tile)
        bias[:, place] = jnp.where(allowed, 0.0, neg_large).astype(f32)
        keep[:, place] = jnp.where(allowed, 1.0, 0.0).astype(f32)
    first_doc = doc_of(base)
    next_doc = doc_of(base + tile)
    after_doc = doc_of(base + 2 * tile)
    in_first = jnp.where(own_doc == first_doc, 1.0, 0.0).astype(f32)
    in_next = jnp.where(own_doc == next_doc, 1.0, 0.0).astype(f32)
    join = jnp.where(next_doc == after_doc, 1.0, 0.0).astype(f32)
    is_even = jnp.where(even, 1.0, 0.0).astype(f32)

    for load in loads[2:]:
        load.wait()
    wide_a[...] = q_ref[...].astype(f32).reshape(tile * heads, width)
    wide_b[...] = do_ref[...].astype(f32).reshape(tile * heads, width)
    for h in range(heads):
        q_h = wide_a[pl.ds(h, tile, stride=heads), :]
        q_own[h] = q_h.astype(bf)
        qm_own[h] = (q_h * in_first).astype(bf)
        do_own[h] = wide_b[pl.ds(h, tile, stride=heads), :].astype(bf)
    sq_acc[...] = jnp.zeros_like(sq_acc)
    pj_acc[...] = jnp.zeros_like(pj_acc)

    @pl.when(me < 2)
    def _():
        win[:, :, 0:tile, :] = jnp.zeros((heads, 2, tile, width), bf)

    @pl.when(me == 0)
    def _():
        win[:, :, tile:2 * tile, :] = jnp.zeros((heads, 2, tile, width), bf)

    @pl.when(me == 1)
    def _():
        rx1[...] = jnp.zeros_like(rx1)

    @pl.when(me >= count - 2)
    def _():
        rx2[...] = jnp.zeros_like(rx2)
        tz[...] = jnp.zeros_like(tz)

    @pl.when(me == count - 1)
    def _():
        tx1[...] = jnp.zeros_like(tx1)

    def pass_on(h):
        part_x(h).wait_recv()
        part2_tx[h] = (part2[h] + rx1[h].astype(f32)).astype(bf)
        part_z(h).start()

    def soft_step(h, carry):
        @pl.when(has_prev)
        def _():
            kv_z(h).wait_recv()

        @pl.when(odd & has_prev)
        def _():
            kv_x_relay(h).start()

        @pl.when(odd | has_prev)
        def _():
            kv_x_own(h).wait_recv()

        q_h, do_h = q_own[h], do_own[h]
        k_w, v_w = win[h, 0], win[h, 1]
        raw = mm(q_h, k_w, NT)
        scores = raw * scale + bias[...]
        top = jnp.max(scores, axis=-1, keepdims=True)
        grown = jnp.exp(scores - top)
        probs = grown * (1.0 / jnp.sum(grown, axis=-1, keepdims=True))
        weights = probs.astype(bf)
        soft_h = mm(weights, v_w, NN)
        att = (raw * keep[...]).astype(bf)
        lin_h = mm(att, v_w, NN)
        grad = do_h.astype(f32)
        row_dot = jnp.sum(grad * soft_h, axis=-1, keepdims=True)
        dscores = (probs * (mm(do_h, v_w, NT) - row_dot)).astype(bf)
        dq[h] = mm(dscores, k_w, NN) * scale
        dk_w = mm(dscores, q_h, TN) * scale
        dv_w = mm(weights, do_h, TN)
        lin[h] = lin_h
        soft[h] = soft_h
        attend[h] = att[:, 2 * tile:]
        dkv[h, 0] = dk_w[2 * tile:]
        dkv[h, 1] = dv_w[2 * tile:]
        part1_tx[h, 0] = dk_w[tile:2 * tile].astype(bf)
        part1_tx[h, 1] = dv_w[tile:2 * tile].astype(bf)
        sq_acc[...] += lin_h * lin_h
        pj_acc[...] += grad * g_ref[pl.ds(h, 1), :] * lin_h

        @pl.when(odd | has_prev)
        def _():
            part_x(h).start()

        @pl.when(even & has_prev)
        def _():
            part2_tx[h, 0] = dk_w[:tile].astype(bf)
            part2_tx[h, 1] = dv_w[:tile].astype(bf)
            part_z(h).start()

        @pl.when(odd & has_prev)
        def _():
            part2[h, 0] = dk_w[:tile]
            part2[h, 1] = dv_w[:tile]

        @pl.when(odd & has_prev & (h >= lag))
        def _():
            pass_on(jnp.maximum(h - lag, 0))

        return carry

    lax.fori_loop(0, heads, soft_step, 0)

    sq_col = jnp.sum(sq_acc[...], axis=-1, keepdims=True)
    pj_col = jnp.sum(pj_acc[...], axis=-1, keepdims=True)
    flat = jnp.where(cols == 0, sq_col, jnp.where(cols == 1, pj_col, 0.0)).T
    stat_tx[...] = flat[:8]
    for k in range(1, groups):
        stats(k).start()

    total = stat_tx[...]
    for k in range(1, groups):
        stats(k).wait_recv()
        total = total + stat_rx[k - 1]
    back_flat = jnp.concatenate([total, jnp.zeros((tile - 8, tile), f32)], axis=0).T
    sq_sum = back_flat[:, 0:1]
    pj_sum = back_flat[:, 1:2]
    inverse = lax.rsqrt(sq_sum / features + norm_eps)
    inv_b[...] = jnp.broadcast_to(inverse, (tile, width))
    coef_b[...] = jnp.broadcast_to(inverse * inverse * inverse * pj_sum / features, (tile, width))

    def state_step(h, carry):
        weighted = do_own[h].astype(f32) * g_ref[pl.ds(h, 1), :]
        inner_h = (inv_b[...] * weighted - lin[h] * coef_b[...]).astype(bf)
        inner[h] = inner_h
        t_tx[h] = mm(qm_own[h], inner_h, TN).astype(bf)

        @pl.when(has_prev)
        def _():
            state_z(h).start()

        @pl.when(odd)
        def _():
            state_x_own(h).start()

        @pl.when(odd & has_prev & (h >= heads - lag))
        def _():
            pass_on(jnp.maximum(h, heads - lag))

        return carry

    lax.fori_loop(0, heads, state_step, 0)

    def local_step(h, carry):
        @pl.when(has_next)
        def _():
            state_z(h).wait_recv()

        @pl.when(even & has_next)
        def _():
            state_x_relay(h).start()

        inner_h = inner[h]
        back = (mm(inner_h, win[h, 1], NT) * keep[...]).astype(bf)
        dq[h] += mm(back, win[h, 0], NN)
        dkv[h, 0] += mm(back[:, 2 * tile:], q_own[h], TN)
        dkv[h, 1] += mm(attend[h], inner_h, TN)
        soft[h] += lin[h] * inv_b[...] * g_ref[pl.ds(h, 1), :]
        return carry

    lax.fori_loop(0, heads, local_step, 0)

    for h in range(heads):
        wide_a[pl.ds(h, tile, stride=heads), :] = soft[h]
        wide_b[pl.ds(h, tile, stride=heads), :] = dq[h]
    mixed_ref[...] = wide_a[...].reshape(tile, heads, width).astype(bf)
    qg_ref[...] = wide_b[...].reshape(tile, heads, width).astype(bf)

    def last_step(h, carry):
        @pl.when(has_next)
        def _():
            part_z(h).wait_recv()

        @pl.when(even)
        def _():
            part_x(h).wait_recv()

        @pl.when(even | has_next)
        def _():
            state_x_own(h).wait_recv()

        state = (tx1[h].astype(f32) + join * tz[h].astype(f32)).astype(bf)
        got = rx1[h].astype(f32) * is_even + rx2[h].astype(f32)
        dkv[h, 0] += got[0] + in_next * mm(win[h, 1, own, :], state, NT)
        dkv[h, 1] += got[1] + in_next * mm(win[h, 0, own, :], state, NN)
        return carry

    lax.fori_loop(0, heads, last_step, 0)

    for h in range(heads):
        wide_a[pl.ds(h, tile, stride=heads), :] = dkv[h, 0]
        wide_b[pl.ds(h, tile, stride=heads), :] = dkv[h, 1]
    kg_ref[...] = wide_a[...].reshape(tile, heads, width).astype(bf)
    vg_ref[...] = wide_b[...].reshape(tile, heads, width).astype(bf)

    def drain(h, carry):
        @pl.when(has_next)
        def _():
            kv_z(h).wait_send()

        @pl.when(even | has_prev)
        def _():
            kv_x_own(h).wait_send()

        @pl.when(odd | has_prev)
        def _():
            part_x(h).wait_send()

        @pl.when(has_prev)
        def _():
            part_z(h).wait_send()
            state_z(h).wait_send()

        @pl.when(odd | has_next)
        def _():
            state_x_own(h).wait_send()

        return carry

    lax.fori_loop(0, heads, drain, 0)
    for k in range(1, groups):
        stats(k).wait_send()


def in_window(queries, keys, values, gain, doc_lengths, cotangent):
    tile, heads, width = queries.shape
    count, groups = lax.axis_size("ctx"), lax.axis_size("head")
    bf, f32 = jnp.bfloat16, jnp.float32
    block = (heads, tile, width)
    pair = (heads, 2, tile, width)
    vmem = pl.BlockSpec(memory_space=pltpu.VMEM)
    each = pltpu.SemaphoreType.DMA((heads,))
    return pl.pallas_call(
        functools.partial(block_kernel, count, groups, heads * groups * width),
        out_shape=[jax.ShapeDtypeStruct(queries.shape, bf)] * 4,
        in_specs=[pl.BlockSpec(memory_space=pltpu.SMEM)] + [pl.BlockSpec(memory_space=pltpu.HBM)] * 5,
        out_specs=[vmem] * 4,
        scratch_shapes=[
            pltpu.VMEM(queries.shape, bf),
            pltpu.VMEM(queries.shape, bf),
            pltpu.VMEM(queries.shape, bf),
            pltpu.VMEM(gain.shape, f32),
            pltpu.VMEM(queries.shape, bf),
            pltpu.SemaphoreType.DMA((5,)),
            pltpu.VMEM((tile * heads, width), f32),
            pltpu.VMEM((tile * heads, width), f32),
            pltpu.VMEM(block, bf),
            pltpu.VMEM(block, bf),
            pltpu.VMEM(block, bf),
            pltpu.VMEM((heads, 2, 3 * tile, width), bf),
            pltpu.VMEM((tile, 3 * tile), f32),
            pltpu.VMEM((tile, 3 * tile), f32),
            pltpu.VMEM((heads, tile, tile), bf),
            pltpu.VMEM(block, f32),
            pltpu.VMEM(block, f32),
            pltpu.VMEM(block, f32),
            pltpu.VMEM(pair, f32),
            pltpu.VMEM(pair, f32),
            pltpu.VMEM(pair, bf),
            pltpu.VMEM(pair, bf),
            pltpu.VMEM(pair, bf),
            pltpu.VMEM(pair, bf),
            pltpu.VMEM(block, bf),
            pltpu.VMEM((heads, width, width), bf),
            pltpu.VMEM((heads, width, width), bf),
            pltpu.VMEM((heads, width, width), bf),
            pltpu.VMEM((tile, width), f32),
            pltpu.VMEM((tile, width), f32),
            pltpu.VMEM((tile, width), f32),
            pltpu.VMEM((tile, width), f32),
            pltpu.VMEM((8, tile), f32),
            pltpu.VMEM((groups - 1, 8, tile), f32),
        ]
        + [each] * 12
        + [pltpu.SemaphoreType.DMA((groups - 1,))] * 2,
        compiler_params=pltpu.CompilerParams(
            collective_id=0, has_side_effects=True, vmem_limit_bytes=63 * 1024 * 1024
        ),
    )(doc_lengths, queries, keys, values, gain, cotangent)


def dispatch(queries, keys, values, gain, doc_lengths, cotangent):
    tile = queries.shape[0]
    count = lax.axis_size("ctx")
    if count * tile <= 4 * SPAN * tile and count % 2 == 0:
        return tuple(in_window(queries, keys, values, gain, doc_lengths, cotangent))
    return per_device(queries, keys, values, gain, doc_lengths, cotangent)


def solution(mesh):
    placed = (
        P("ctx", "head", None),
        P("ctx", "head", None),
        P("ctx", "head", None),
        P("head", None),
        P(),
        P("ctx", "head", None),
    )
    return jax.shard_map(
        dispatch,
        mesh=mesh,
        in_specs=placed,
        out_specs=(
            P("ctx", "head", None),
            P("ctx", "head", None),
            P("ctx", "head", None),
            P("ctx", "head", None),
        ),
        check_vma=False,
    )
```

```python
import functools

import jax
import jax.numpy as jnp
from jax import lax
from jax.experimental import pallas as pl
from jax.experimental.pallas import tpu as pltpu
from jax.sharding import PartitionSpec as P

SPAN = 2


neg_large = -1e30
norm_eps = 1e-06


def from_behind(x, axis, by):
    devices = lax.axis_size(axis)
    pairs = [(i, i + by) for i in range(devices) if 0 <= i + by < devices]
    return lax.ppermute(x, axis, pairs)


def carried_in(part, axis, combine, reverse):
    count = lax.axis_size(axis)
    sign = -1 if reverse else 1

    def moved(part, by):
        return jax.tree.map(lambda a: from_behind(a, axis, sign * by), part)

    state, by = moved(part, 1), 1
    while by < count:
        state = combine(moved(state, by), state)
        by *= 2
    return state


def over_heads(x):
    groups = lax.axis_size("head")
    total = x
    for by in range(1, groups):
        pairs = [(i, (i + by) % groups) for i in range(groups)]
        total = total + lax.ppermute(x, "head", pairs)
    return total


def wide(form, left, right):
    return jnp.einsum(form, left, right, precision=lax.Precision.HIGHEST)


def narrow(form, left, right):
    return jnp.einsum(form, left, right, preferred_element_type=jnp.float32)


def doc_index(doc_lengths, positions):
    order = jnp.arange(doc_lengths.shape[0])
    starts = jnp.sum(jnp.where(order[None, :] < order[:, None], doc_lengths[None, :], 0), axis=1)
    return jnp.sum((starts[None, :] <= positions[:, None]).astype(jnp.int32), axis=1) - 1


def one_doc(doc_lengths, position):
    return doc_index(doc_lengths, jnp.reshape(position, (1,)))[0]


def join_states(earlier, later):
    return (later[0] + (1.0 - later[1]) * earlier[0], jnp.maximum(earlier[1], later[1]))


def masked_scores(query_block, key_block, mask, scale):
    raw = narrow("thd,uhd->htu", query_block, key_block) * scale
    return jnp.where(mask[None], raw, neg_large)


def key_terms(dscores, weights, query_block, grad_block, scale):
    key_part = narrow("htu,thd->uhd", dscores, query_block) * scale
    value_part = narrow("htu,thd->uhd", weights, grad_block)
    return (key_part, value_part)


def per_device(queries, keys, values, gain, doc_lengths, cotangent):
    tile, heads, width = queries.shape
    features = heads * lax.axis_size("head") * width
    scale = width ** (-0.5)
    base = lax.axis_index("ctx") * tile
    offsets = jnp.arange(tile, dtype=jnp.int32)
    own_pos = base + offsets
    own_doc = doc_index(doc_lengths, own_pos)
    prev_doc = one_doc(doc_lengths, base - 1)
    next_doc = one_doc(doc_lengths, base + tile)
    pair = jnp.stack([keys, values])
    arrived = [from_behind(pair, "ctx", shift) for shift in range(SPAN, 0, -1)]
    key_tiles = [piece[0] for piece in arrived] + [keys]
    value_tiles = [piece[1] for piece in arrived] + [values]
    masks = []
    for position in range(SPAN + 1):
        key_pos = base - (SPAN - position) * tile + offsets
        key_doc = doc_index(doc_lengths, key_pos)
        masks.append(
            (own_doc[:, None] == key_doc[None, :]) & (key_pos[None, :] <= own_pos[:, None])
        )
    score_list = [
        masked_scores(queries, key_tiles[position], masks[position], scale)
        for position in range(SPAN + 1)
    ]
    top = score_list[0].max(axis=-1)
    for position in range(1, SPAN + 1):
        top = jnp.maximum(top, score_list[position].max(axis=-1))
    total = jnp.zeros((heads, tile), jnp.float32)
    for position in range(SPAN + 1):
        total = total + jnp.sum(jnp.exp(score_list[position] - top[..., None]), axis=-1)
    log_total = top + jnp.log(total)
    prob_list = []
    weight_list = []
    soft_out = jnp.zeros((tile, heads, width), jnp.float32)
    for position in range(SPAN + 1):
        probs = jnp.exp(score_list[position] - log_total[..., None])
        weights = probs.astype(jnp.bfloat16)
        prob_list.append(probs)
        weight_list.append(weights)
        soft_out = soft_out + narrow("htu,uhd->thd", weights, value_tiles[position])
    same_tile = masks[SPAN].astype(jnp.float32)
    carried_prev = (own_doc == prev_doc).astype(jnp.float32)
    carried_next = (own_doc == next_doc).astype(jnp.float32)
    keep_last = (own_doc == own_doc[tile - 1])[:, None, None]
    keep_first = (own_doc == own_doc[0])[:, None, None]
    reset_front = (prev_doc != own_doc[tile - 1]).astype(jnp.float32)
    reset_back = (next_doc != own_doc[0]).astype(jnp.float32)
    query_wide = queries.astype(jnp.float32)
    attend = (narrow("thd,uhd->htu", queries, keys) * same_tile).astype(jnp.bfloat16)
    local_state = narrow("uhd,uhe->hde", jnp.where(keep_last, keys, jnp.zeros_like(keys)), values)
    incoming, front_flag = carried_in(
        (local_state, reset_front), "ctx", join_states, False
    )
    linear_out = (
        narrow("htu,uhd->thd", attend, values)
        + wide("thd,hde->the", query_wide, incoming) * carried_prev[:, None, None]
    )
    squares = over_heads(jnp.sum(linear_out * linear_out, axis=(1, 2)))
    inverse = lax.rsqrt(squares / features + norm_eps)
    mixed = (linear_out * inverse[:, None, None] * gain[None] + soft_out).astype(jnp.bfloat16)
    grad_wide = cotangent.astype(jnp.float32)
    weighted = grad_wide * gain[None]
    projection = over_heads(jnp.sum(weighted * linear_out, axis=(1, 2)))
    inner = (
        inverse[:, None, None] * weighted
        - linear_out * (inverse**3 * projection / features)[:, None, None]
    ).astype(jnp.bfloat16)
    row_dot = jnp.sum(grad_wide * soft_out, axis=-1).T
    query_soft = jnp.zeros((tile, heads, width), jnp.float32)
    dscore_list = []
    for position in range(SPAN + 1):
        dprobs = narrow("thd,uhd->htu", cotangent, value_tiles[position])
        dscores = (prob_list[position] * (dprobs - row_dot[..., None])).astype(jnp.bfloat16)
        query_soft = query_soft + narrow("htu,uhd->thd", dscores, key_tiles[position]) * scale
        dscore_list.append(dscores)
    inner_wide = inner.astype(jnp.float32)
    back = (narrow("thd,uhd->htu", inner, values) * same_tile).astype(jnp.bfloat16)
    query_linear = (
        narrow("htu,uhd->thd", back, keys)
        + wide("the,hde->thd", inner_wide, incoming) * carried_prev[:, None, None]
    )
    tile_sum = narrow(
        "thd,the->hde", jnp.where(keep_first, queries, jnp.zeros_like(queries)), inner
    )
    later, back_flag = carried_in(
        (tile_sum, reset_back), "ctx", join_states, True
    )
    key_linear = (
        narrow("htu,thd->uhd", back, queries)
        + wide("uhe,hde->uhd", values.astype(jnp.float32), later) * carried_next[:, None, None]
    )
    value_linear = (
        narrow("htu,the->uhe", attend, inner)
        + wide("uhd,hde->uhe", keys.astype(jnp.float32), later) * carried_next[:, None, None]
    )
    parts = [
        key_terms(dscore_list[position], weight_list[position], queries, cotangent, scale)
        for position in range(SPAN + 1)
    ]
    key_soft, value_soft = parts[SPAN]
    for shift in range(1, SPAN + 1):
        sent = jnp.stack([parts[SPAN - shift][0], parts[SPAN - shift][1]])
        returned = from_behind(sent.astype(jnp.bfloat16), "ctx", -shift).astype(sent.dtype)
        key_soft = key_soft + returned[0]
        value_soft = value_soft + returned[1]
    query_grad = (query_linear + query_soft).astype(jnp.bfloat16)
    key_grad = (key_linear + key_soft).astype(jnp.bfloat16)
    value_grad = (value_linear + value_soft).astype(jnp.bfloat16)
    return (mixed, query_grad, key_grad, value_grad)


def mm(left, right, dims):
    return lax.dot_general(left, right, (dims, ((), ())), preferred_element_type=jnp.float32)


NT = ((1,), (1,))
NN = ((1,), (0,))
TN = ((0,), (0,))


def block_kernel(
    count, groups, features,
    len_ref, q_hbm, k_hbm, v_hbm, g_hbm, do_hbm,
    mixed_ref, qg_ref, kg_ref, vg_ref,
    q_ref, k_ref, v_ref, g_ref, do_ref, in_sem,
    wide_a, wide_b, q_own, do_own, win, bias, keep, attend, lin, soft,
    dq, dkv, part1_tx, part2_tx, rx1, rx2,
    sq_acc, pj_acc, inv_b, coef_b, stat_tx, stat_rx,
    kvz_s, kvz_r, kvx_s, kvx_r, pz_s, pz_r, px_s, px_r, st_s, st_r,
):
    heads, tile, width = q_own.shape
    scale = width ** (-0.5)
    bf = jnp.bfloat16
    f32 = jnp.float32
    me = lax.axis_index("ctx")
    group = lax.axis_index("head")
    odd = lax.rem(me, 2) == 1
    even = lax.rem(me, 2) == 0
    has_prev = me >= 2
    has_next = me < count - 2
    side = me + 1 - 2 * lax.rem(me, 2)
    lag = 2

    def remote(src, dst, send, recv, axis, to):
        return pltpu.make_async_remote_copy(
            src_ref=src, dst_ref=dst, send_sem=send, recv_sem=recv,
            device_id={axis: to}, device_id_type=pl.DeviceIdType.MESH,
        )

    old, mid, own = pl.ds(0, tile), pl.ds(tile, tile), pl.ds(2 * tile, tile)

    def kv_z(h):
        return remote(win.at[h, :, own], win.at[h, :, old], kvz_s.at[h], kvz_r.at[h], "ctx", me + 2)

    def kv_x_own(h):
        return remote(win.at[h, :, own], win.at[h, :, mid], kvx_s.at[h], kvx_r.at[h], "ctx", side)

    def kv_x_relay(h):
        return remote(win.at[h, :, old], win.at[h, :, mid], kvx_s.at[h], kvx_r.at[h], "ctx", side)

    def part_x(h):
        return remote(part1_tx.at[h], rx1.at[h], px_s.at[h], px_r.at[h], "ctx", side)

    def part_z(h):
        return remote(part2_tx.at[h], rx2.at[h], pz_s.at[h], pz_r.at[h], "ctx", me - 2)

    def stats(k):
        return remote(
            stat_tx, stat_rx.at[k - 1], st_s.at[k - 1], st_r.at[k - 1], "head",
            lax.rem(group + k, groups),
        )

    def greet(axis, to):
        pl.semaphore_signal(
            barrier, inc=1, device_id={axis: to}, device_id_type=pl.DeviceIdType.MESH
        )

    loads = [
        pltpu.make_async_copy(source, target, in_sem.at[n])
        for n, (source, target) in enumerate(
            [(k_hbm, k_ref), (v_hbm, v_ref), (q_hbm, q_ref), (do_hbm, do_ref), (g_hbm, g_ref)]
        )
    ]
    for load in loads:
        load.start()
    barrier = pltpu.get_barrier_semaphore()
    greet("ctx", side)
    for k in range(1, groups):
        greet("head", lax.rem(group + k, groups))

    @pl.when(has_prev)
    def _():
        greet("ctx", me - 2)

    @pl.when(has_next)
    def _():
        greet("ctx", me + 2)

    loads[0].wait()
    loads[1].wait()
    wide_a[...] = k_ref[...].astype(f32).reshape(tile * heads, width)
    wide_b[...] = v_ref[...].astype(f32).reshape(tile * heads, width)
    for h in range(heads):
        win[h, 0, 2 * tile:3 * tile, :] = wide_a[pl.ds(h, tile, stride=heads), :].astype(bf)
        win[h, 1, 2 * tile:3 * tile, :] = wide_b[pl.ds(h, tile, stride=heads), :].astype(bf)

    pl.semaphore_wait(barrier, groups + has_prev.astype(jnp.int32) + has_next.astype(jnp.int32))

    def send_kv(h, carry):
        @pl.when(has_next)
        def _():
            kv_z(h).start()

        @pl.when(even)
        def _():
            kv_x_own(h).start()

        return carry

    lax.fori_loop(0, heads, send_kv, 0)

    starts = []
    running = jnp.int32(0)
    for d in range(len_ref.shape[0]):
        starts.append(running)
        running = running + len_ref[d]
    base = me * tile

    def doc_of(position):
        total = jnp.zeros_like(position)
        for start in starts:
            total = total + jnp.where(position >= start, 1, 0).astype(jnp.int32)
        return total

    rows = lax.broadcasted_iota(jnp.int32, (tile, tile), 0)
    cols = lax.broadcasted_iota(jnp.int32, (tile, tile), 1)
    own_pos = base + rows
    own_doc = doc_of(own_pos)
    for position in range(3):
        key_pos = base - (2 - position) * tile + cols
        allowed = (own_doc == doc_of(key_pos)) & (key_pos <= own_pos)
        place = slice(position * tile, (position + 1) * tile)
        bias[:, place] = jnp.where(allowed, 0.0, neg_large).astype(f32)
        keep[:, place] = jnp.where(allowed, 1.0, 0.0).astype(f32)
    is_even = jnp.where(even, 1.0, 0.0).astype(f32)

    for load in loads[2:]:
        load.wait()
    wide_a[...] = q_ref[...].astype(f32).reshape(tile * heads, width)
    wide_b[...] = do_ref[...].astype(f32).reshape(tile * heads, width)
    for h in range(heads):
        q_h = wide_a[pl.ds(h, tile, stride=heads), :]
        q_own[h] = q_h.astype(bf)
        do_own[h] = wide_b[pl.ds(h, tile, stride=heads), :].astype(bf)
    sq_acc[...] = jnp.zeros_like(sq_acc)
    pj_acc[...] = jnp.zeros_like(pj_acc)

    @pl.when(me < 2)
    def _():
        win[:, :, 0:tile, :] = jnp.zeros((heads, 2, tile, width), bf)

    @pl.when(me == 0)
    def _():
        win[:, :, tile:2 * tile, :] = jnp.zeros((heads, 2, tile, width), bf)

    @pl.when(me == 1)
    def _():
        rx1[...] = jnp.zeros_like(rx1)

    @pl.when(me >= count - 2)
    def _():
        rx2[...] = jnp.zeros_like(rx2)

    def pass_on(h):
        part_x(h).wait_recv()
        part2_tx[h] = (dkv[h, :, 0:tile, :] + rx1[h].astype(f32)).astype(bf)
        part_z(h).start()

    def soft_step(h, carry):
        @pl.when(has_prev)
        def _():
            kv_z(h).wait_recv()

        @pl.when(odd & has_prev)
        def _():
            kv_x_relay(h).start()

        @pl.when(odd | has_prev)
        def _():
            kv_x_own(h).wait_recv()

        q_h, do_h = q_own[h], do_own[h]
        k_w, v_w = win[h, 0], win[h, 1]
        raw = mm(q_h, k_w, NT)
        scores = raw * scale + bias[...]
        top = jnp.max(scores, axis=-1, keepdims=True)
        grown = jnp.exp(scores - top)
        probs = grown * (1.0 / jnp.sum(grown, axis=-1, keepdims=True))
        weights = probs.astype(bf)
        soft_h = mm(weights, v_w, NN)
        att = (raw * keep[...]).astype(bf)
        lin_h = mm(att, v_w, NN)
        grad = do_h.astype(f32)
        row_dot = jnp.sum(grad * soft_h, axis=-1, keepdims=True)
        dscores = (probs * (mm(do_h, v_w, NT) - row_dot)).astype(bf)
        dq[h] = mm(dscores, k_w, NN) * scale
        dkv[h, 0] = mm(dscores, q_h, TN) * scale
        dkv[h, 1] = mm(weights, do_h, TN)
        lin[h] = lin_h
        soft[h] = soft_h
        attend[h] = att
        sq_acc[...] += lin_h * lin_h
        pj_acc[...] += grad * g_ref[pl.ds(h, 1), :] * lin_h

        return carry

    lax.fori_loop(0, heads, soft_step, 0)

    sq_col = jnp.sum(sq_acc[...], axis=-1, keepdims=True)
    pj_col = jnp.sum(pj_acc[...], axis=-1, keepdims=True)
    flat = jnp.where(cols == 0, sq_col, jnp.where(cols == 1, pj_col, 0.0)).T
    stat_tx[...] = flat[:8]
    for k in range(1, groups):
        stats(k).start()

    total = stat_tx[...]
    for k in range(1, groups):
        stats(k).wait_recv()
        total = total + stat_rx[k - 1]
    back_flat = jnp.concatenate([total, jnp.zeros((tile - 8, tile), f32)], axis=0).T
    sq_sum = back_flat[:, 0:1]
    pj_sum = back_flat[:, 1:2]
    inverse = lax.rsqrt(sq_sum / features + norm_eps)
    inv_b[...] = jnp.broadcast_to(inverse, (tile, width))
    coef_b[...] = jnp.broadcast_to(inverse * inverse * inverse * pj_sum / features, (tile, width))

    def linear_step(h, carry):
        weighted = do_own[h].astype(f32) * g_ref[pl.ds(h, 1), :]
        lin_h = lin[h]
        inner_h = (inv_b[...] * weighted - lin_h * coef_b[...]).astype(bf)
        back = (mm(inner_h, win[h, 1], NT) * keep[...]).astype(bf)
        dkv[h, 0] += mm(back, q_own[h], TN)
        dkv[h, 1] += mm(attend[h], inner_h, TN)

        @pl.when(odd | has_prev)
        def _():
            part1_tx[h] = dkv[h, :, tile:2 * tile, :].astype(bf)
            part_x(h).start()

        @pl.when(even & has_prev)
        def _():
            part2_tx[h] = dkv[h, :, 0:tile, :].astype(bf)
            part_z(h).start()

        @pl.when(odd & has_prev & (h >= lag))
        def _():
            pass_on(jnp.maximum(h - lag, 0))

        dq[h] += mm(back, win[h, 0], NN)
        soft[h] += lin_h * inv_b[...] * g_ref[pl.ds(h, 1), :]
        return carry

    lax.fori_loop(0, heads, linear_step, 0)

    @pl.when(odd & has_prev)
    def _():
        lax.fori_loop(heads - lag, heads, lambda h, c: (pass_on(h), c)[1], 0)

    for h in range(heads):
        wide_a[pl.ds(h, tile, stride=heads), :] = soft[h]
        wide_b[pl.ds(h, tile, stride=heads), :] = dq[h]
    mixed_ref[...] = wide_a[...].reshape(tile, heads, width).astype(bf)
    qg_ref[...] = wide_b[...].reshape(tile, heads, width).astype(bf)

    def last_step(h, carry):
        @pl.when(has_next)
        def _():
            part_z(h).wait_recv()

        @pl.when(even)
        def _():
            part_x(h).wait_recv()

        got = rx1[h].astype(f32) * is_even + rx2[h].astype(f32)
        dkv[h, :, 2 * tile:3 * tile, :] += got
        return carry

    lax.fori_loop(0, heads, last_step, 0)

    for h in range(heads):
        wide_a[pl.ds(h, tile, stride=heads), :] = dkv[h, 0, 2 * tile:3 * tile, :]
        wide_b[pl.ds(h, tile, stride=heads), :] = dkv[h, 1, 2 * tile:3 * tile, :]
    kg_ref[...] = wide_a[...].reshape(tile, heads, width).astype(bf)
    vg_ref[...] = wide_b[...].reshape(tile, heads, width).astype(bf)

    def drain(h, carry):
        @pl.when(has_next)
        def _():
            kv_z(h).wait_send()

        @pl.when(even | has_prev)
        def _():
            kv_x_own(h).wait_send()

        @pl.when(odd | has_prev)
        def _():
            part_x(h).wait_send()

        @pl.when(has_prev)
        def _():
            part_z(h).wait_send()

        return carry

    lax.fori_loop(0, heads, drain, 0)
    for k in range(1, groups):
        stats(k).wait_send()


def in_window(queries, keys, values, gain, doc_lengths, cotangent):
    tile, heads, width = queries.shape
    count, groups = lax.axis_size("ctx"), lax.axis_size("head")
    bf, f32 = jnp.bfloat16, jnp.float32
    block = (heads, tile, width)
    pair = (heads, 2, tile, width)
    vmem = pl.BlockSpec(memory_space=pltpu.VMEM)
    each = pltpu.SemaphoreType.DMA((heads,))
    return pl.pallas_call(
        functools.partial(block_kernel, count, groups, heads * groups * width),
        out_shape=[jax.ShapeDtypeStruct(queries.shape, bf)] * 4,
        in_specs=[pl.BlockSpec(memory_space=pltpu.SMEM)] + [pl.BlockSpec(memory_space=pltpu.HBM)] * 5,
        out_specs=[vmem] * 4,
        scratch_shapes=[
            pltpu.VMEM(queries.shape, bf),
            pltpu.VMEM(queries.shape, bf),
            pltpu.VMEM(queries.shape, bf),
            pltpu.VMEM(gain.shape, f32),
            pltpu.VMEM(queries.shape, bf),
            pltpu.SemaphoreType.DMA((5,)),
            pltpu.VMEM((tile * heads, width), f32),
            pltpu.VMEM((tile * heads, width), f32),
            pltpu.VMEM(block, bf),
            pltpu.VMEM(block, bf),
            pltpu.VMEM((heads, 2, 3 * tile, width), bf),
            pltpu.VMEM((tile, 3 * tile), f32),
            pltpu.VMEM((tile, 3 * tile), f32),
            pltpu.VMEM((heads, tile, 3 * tile), bf),
            pltpu.VMEM(block, f32),
            pltpu.VMEM(block, f32),
            pltpu.VMEM(block, f32),
            pltpu.VMEM((heads, 2, 3 * tile, width), f32),
            pltpu.VMEM(pair, bf),
            pltpu.VMEM(pair, bf),
            pltpu.VMEM(pair, bf),
            pltpu.VMEM(pair, bf),
            pltpu.VMEM((tile, width), f32),
            pltpu.VMEM((tile, width), f32),
            pltpu.VMEM((tile, width), f32),
            pltpu.VMEM((tile, width), f32),
            pltpu.VMEM((8, tile), f32),
            pltpu.VMEM((groups - 1, 8, tile), f32),
        ]
        + [each] * 8
        + [pltpu.SemaphoreType.DMA((groups - 1,))] * 2,
        compiler_params=pltpu.CompilerParams(
            collective_id=0, has_side_effects=True, vmem_limit_bytes=63 * 1024 * 1024
        ),
    )(doc_lengths, queries, keys, values, gain, cotangent)


def dispatch(queries, keys, values, gain, doc_lengths, cotangent):
    tile = queries.shape[0]
    count = lax.axis_size("ctx")
    if count * tile <= 4 * SPAN * tile and count % 2 == 0:
        return tuple(in_window(queries, keys, values, gain, doc_lengths, cotangent))
    return per_device(queries, keys, values, gain, doc_lengths, cotangent)


def solution(mesh):
    placed = (
        P("ctx", "head", None),
        P("ctx", "head", None),
        P("ctx", "head", None),
        P("head", None),
        P(),
        P("ctx", "head", None),
    )
    return jax.shard_map(
        dispatch,
        mesh=mesh,
        in_specs=placed,
        out_specs=(
            P("ctx", "head", None),
            P("ctx", "head", None),
            P("ctx", "head", None),
            P("ctx", "head", None),
        ),
        check_vma=False,
    )
```
